32 devices in a mesh: section: 4 (over y, x), row: 2 (over core), col: 4 (over z).
Axes of the slice: x: 2, y: 2, z: 4, core: 2. Of those that a mesh axis runs over, the one named last changes fastest.
Arguments:
- inputs: bfloat16 [4, 128, 4096], P('section', 'col', 'row'), may hold values from -6 to 6
- gate_pre: bfloat16 [4, 128, 14336], P('section', None, 'col'), may hold values from -8 to 8
- up_weight: bfloat16 [4096, 14336], P('row', 'col'), may hold values from -0.09375 to 0.09375
- down_weight: bfloat16 [14336, 4096], P('col', 'row'), may hold values from -0.046875 to 0.046875
- output_grad: bfloat16 [4, 128, 4096], P('section', 'col', 'row'), may hold values from -6 to 6
Outputs:
- handed_forward: bfloat16 [4, 128, 4096], P('section', 'col', 'row')
- gate_grad: bfloat16 [4, 128, 14336], P('section', 'row', 'col')
- handed_back: bfloat16 [4, 128, 4096], P('section', 'col', 'row')
The draws below stay inside these ranges and needn't reach their ends.
All inputs are finite; a program needn't handle non-finite values.
Results may differ from the reference program's by a relative error of at most 0.0041.
Values may be sent and summed in bfloat16 or wider, within the bound.
No kernel may reach another device: no remote copies, remote signals or barrier semaphores. Data moves between devices by JAX's collectives and lax.ppermute only.
A program may use at most 64 MiB of HBM per device.

```python
import jax
import jax.numpy as jnp

D = 4096
FF = 14336
TOK = 128
SECTIONS = 4


def level_of(key, extent, cuts, least, high):
    gain = 1.0
    for position, parts in cuts:
        heights = jax.random.uniform(jax.random.fold_in(jax.random.fold_in(key, 6), position), (parts,), jnp.float32, least / len(cuts), high / len(cuts))
        gain = gain * jnp.repeat(jnp.exp(heights), extent[position] // parts).reshape((-1,) + (1,) * (len(extent) - 1 - position))
    return gain


def gaussian(stream_key, shape, scale, reach, split=(), held_as=jnp.bfloat16):
    values = scale * jax.random.normal(stream_key, shape, jnp.float32)
    if split:
        values = values * level_of(stream_key, shape, split, -0.22, 0.18)
    return jnp.clip(values, -reach, reach).astype(held_as)


def setup_inputs(seed: int = 0) -> dict:
    key_list = jax.random.split(jax.random.key(seed), 6)
    inputs = gaussian(key_list[0], (SECTIONS, TOK, D), 1.0, 6.0, ((0, 4), (1, 4), (2, 2)))
    gate_pre = gaussian(key_list[1], (SECTIONS, TOK, FF), 1.5, 8.0, ((0, 4), (2, 4)))
    up_weight = gaussian(key_list[2], (D, FF), D ** -0.5, 0.09375, ((0, 2), (1, 4)))
    down_weight = gaussian(key_list[3], (FF, D), FF ** -0.5, 0.046875, ((0, 4), (1, 2)))
    output_grad = gaussian(key_list[4], (SECTIONS, TOK, D), 1.0, 6.0, ((0, 4), (1, 4), (2, 2)))
    return dict(inputs=inputs, gate_pre=gate_pre, up_weight=up_weight, down_weight=down_weight, output_grad=output_grad)


def reference(inputs, gate_pre, up_weight, down_weight, output_grad):
    replicas, tokens, width = inputs.shape
    flat_in = inputs.reshape(replicas * tokens, width)
    flat_grad = output_grad.reshape(replicas * tokens, width)
    gate_full = gate_pre.reshape(replicas * tokens, -1).astype(jnp.float32)
    up_act = jnp.dot(flat_in, up_weight, preferred_element_type=jnp.float32)
    sigmoid_gate = jax.nn.sigmoid(gate_full)
    hidden = (gate_full * sigmoid_gate * up_act).astype(jnp.bfloat16)
    mixed = jnp.dot(hidden, down_weight, preferred_element_type=jnp.float32)
    layer_out = (flat_in.astype(jnp.float32) + mixed).astype(jnp.bfloat16)
    hidden_grad = jnp.dot(flat_grad, down_weight.T, preferred_element_type=jnp.float32)
    up_grad = (hidden_grad * gate_full * sigmoid_gate).astype(jnp.bfloat16)
    gate_grad = (hidden_grad * up_act * sigmoid_gate * (1.0 + gate_full * (1.0 - sigmoid_gate))).astype(jnp.bfloat16)
    back_sum = jnp.dot(up_grad, up_weight.T, preferred_element_type=jnp.float32)
    input_grad = (flat_grad.astype(jnp.float32) + back_sum).astype(jnp.bfloat16)
    layer_out = layer_out.reshape(replicas, tokens, width)
    input_grad = input_grad.reshape(replicas, tokens, width)
    handed_forward = jnp.roll(layer_out, 1, axis=0)
    handed_back = jnp.roll(input_grad, -1, axis=0)
    return handed_forward, gate_grad.reshape(replicas, tokens, -1), handed_back
```

```python
import functools

import jax
import jax.numpy as jnp
from jax import lax
from jax.experimental import pallas as pl
from jax.experimental.pallas import tpu as pltpu
from jax.sharding import PartitionSpec as P

MIB = 1 << 20
VMEM = pl.BlockSpec(memory_space=pltpu.VMEM)
SMEM = pl.BlockSpec(memory_space=pltpu.SMEM)
F32 = jnp.float32
BF16 = jnp.bfloat16


def spans(extent, width):
    return [(start, min(width, extent - start)) for start in range(0, extent, width)]


def halves(extent):
    first = -(-extent // 256) * 128
    return [(0, first), (first, extent - first)]


def kernel_call(body, name, outs, args, flops=0, scratch=(), limit=12 * MIB, smem=0):
    moved = sum(a.size * a.dtype.itemsize for a in args)
    return pl.pallas_call(
        body,
        name=name,
        out_shape=outs,
        in_specs=[SMEM] * smem + [VMEM] * (len(args) - smem),
        out_specs=[VMEM] * len(outs),
        scratch_shapes=list(scratch),
        compiler_params=pltpu.CompilerParams(vmem_limit_bytes=limit),
        cost_estimate=pl.CostEstimate(flops=flops, bytes_accessed=moved, transcendentals=0),
    )(*args)


def shape(dims, dtype):
    return jax.ShapeDtypeStruct(tuple(dims), dtype)


def gates(place, gate, row_count):
    tokens, hidden = gate.shape
    own = tokens // row_count

    def body(place_ref, gate_ref, silu_ref, slope_ref):
        start = pl.multiple_of(place_ref[1] * own, own)
        for at, wide in spans(hidden, 512):
            value = gate_ref[:, at : at + wide].astype(F32)
            sig = 1.0 / (1.0 + jnp.exp(-value))
            silu_ref[:, at : at + wide] = value * sig
            value = gate_ref[pl.ds(start, own), at : at + wide].astype(F32)
            sig = 1.0 / (1.0 + jnp.exp(-value))
            slope_ref[:, at : at + wide] = sig * (1.0 + value * (1.0 - sig))

    return kernel_call(
        body,
        "gates",
        [shape((tokens, hidden), F32), shape((own, hidden), F32)],
        [place, gate],
        smem=1,
    )


def first_product(place, pieces, weight, part, weight_rows, name):
    gathered = not isinstance(pieces, list)
    at0, wide0 = part
    inner = weight.shape[1] if weight_rows else weight.shape[0]

    def multiply(tokens_ref, weight_ref, out_ref):
        for at, wide in spans(wide0, 256):
            cut = slice(at0 + at, at0 + at + wide)
            if weight_rows:
                value = lax.dot_general(
                    weight_ref[cut, :], tokens_ref[...], (((1,), (1,)), ((), ())), preferred_element_type=F32
                ).T
            else:
                value = jnp.dot(tokens_ref[...], weight_ref[:, cut], preferred_element_type=F32)
            out_ref[:, at : at + wide] = value

    if gathered:
        tokens = pieces.shape[0]

        def body(tokens_ref, weight_ref, out_ref):
            multiply(tokens_ref, weight_ref, out_ref)

        return kernel_call(
            body, name, [shape((tokens, wide0), F32)], [pieces, weight], flops=2 * tokens * inner * wide0
        )[0]

    count = len(pieces)
    rows = pieces[0].shape[0]
    tokens = rows * count
    direct = rows % 16 == 0

    def body(place_ref, *refs):
        piece_refs, (weight_ref, out_ref, tokens_ref), scratch = refs[:count], refs[count : count + 3], refs[count + 3 :]
        held = tokens_ref if direct else scratch[0]
        for k in range(count):
            at = pl.multiple_of(lax.bitwise_xor(place_ref[0], k) * rows, rows)
            held[pl.ds(at, rows), :] = piece_refs[k][...].astype(held.dtype)
        if not direct:
            tokens_ref[...] = held[...].astype(BF16)
        multiply(tokens_ref, weight_ref, out_ref)

    return kernel_call(
        body,
        name,
        [shape((tokens, wide0), F32), shape((tokens, inner), BF16)],
        [place] + pieces + [weight],
        flops=2 * tokens * inner * wide0,
        scratch=[] if direct else [pltpu.VMEM((tokens, inner), F32)],
        smem=1,
    )


def blend(silu, mine, theirs, parts, name):
    tokens, hidden = silu.shape
    count = len(parts)

    def body(silu_ref, *refs):
        out_ref = refs[-1]
        for k, (at0, wide0) in enumerate(parts):
            for at, wide in spans(wide0, 256):
                total = refs[k][:, at : at + wide] + refs[count + k][:, at : at + wide]
                out_ref[:, at0 + at : at0 + at + wide] = (silu_ref[:, at0 + at : at0 + at + wide] * total).astype(BF16)

    return kernel_call(body, name, [shape((tokens, hidden), BF16)], [silu] + mine + theirs)[0]


def second_product(place, values, weight, residual, part, weight_rows, blocks, name):
    tokens, hidden = values.shape
    rows = tokens // blocks
    at0, wide0 = part

    def body(place_ref, values_ref, weight_ref, residual_ref, *refs):
        outs, total_ref = refs[:blocks], refs[blocks]
        for at, wide in spans(wide0, 256):
            cut = slice(at0 + at, at0 + at + wide)
            if weight_rows:
                total = lax.dot_general(
                    weight_ref[cut, :], values_ref[...], (((1,), (1,)), ((), ())), preferred_element_type=F32
                ).T
            else:
                total = jnp.dot(values_ref[...], weight_ref[:, cut], preferred_element_type=F32)
            total_ref[:, at : at + wide] = total
        for k in range(blocks):
            start = pl.multiple_of(lax.bitwise_xor(place_ref[0], k) * rows, rows)
            piece = total_ref[pl.ds(start, rows), :]
            if k == 0:
                piece = piece + residual_ref[:, at0 : at0 + wide0].astype(F32)
            outs[k][...] = piece.astype(BF16)

    return kernel_call(
        body,
        name,
        [shape((rows, wide0), BF16)] * blocks,
        [place, values, weight, residual],
        flops=2 * tokens * hidden * wide0,
        scratch=[pltpu.VMEM((tokens, wide0), F32)],
        smem=1,
    )


def gate_gradient(place, slope, up_mine, up_theirs, back_mine, back_theirs, parts):
    own, hidden = slope.shape
    count = len(parts)

    def body(place_ref, slope_ref, *refs):
        out_ref = refs[-1]
        start = pl.multiple_of(place_ref[1] * own, own)
        rows = pl.ds(start, own)
        for k, (at0, wide0) in enumerate(parts):
            for at, wide in spans(wide0, 256):
                cut = slice(at, at + wide)
                up = refs[k][rows, cut] + refs[count + k][rows, cut]
                back = refs[2 * count + k][rows, cut] + refs[3 * count + k][rows, cut]
                whole = slice(at0 + at, at0 + at + wide)
                out_ref[:, whole] = (back * up * slope_ref[:, whole]).astype(BF16)

    return kernel_call(
        body,
        "gate_gradient",
        [shape((own, hidden), BF16)],
        [place, slope] + up_mine + up_theirs + back_mine + back_theirs,
        smem=1,
    )[0]


def collect(pieces, name):
    rows = pieces[0][0].shape[0]
    widths = [part[0].shape[1] for part in pieces]
    blocks = len(pieces[0])

    def body(*refs):
        out_ref = refs[-1]
        at = 0
        for p, wide in enumerate(widths):
            total = refs[p * blocks][...].astype(F32)
            for k in range(1, blocks):
                total = total + refs[p * blocks + k][...].astype(F32)
            out_ref[:, at : at + wide] = total.astype(BF16)
            at += wide

    return kernel_call(body, name, [shape((rows, sum(widths)), BF16)], [a for part in pieces for a in part])[0]


def shards(sections, cols, row_count, inputs, gate_pre, up_weight, down_weight, output_grad):
    own_x, own_g, gate = inputs[0], output_grad[0], gate_pre[0]
    place = jnp.stack([lax.axis_index("col"), lax.axis_index("row")]).astype(jnp.int32)

    def from_xor(value, k):
        return lax.ppermute(value, "col", [(c, c ^ k) for c in range(cols)])

    def to_block(value, k, step):
        pairs = [
            (s * cols + c, (s + step) % sections * cols + (c ^ k)) for s in range(sections) for c in range(cols)
        ]
        return lax.ppermute(value, ("section", "col"), pairs)

    def other_row(value):
        return lax.ppermute(value, "row", [(r, (r + 1) % row_count) for r in range(row_count)])

    hidden = gate.shape[1]
    hidden_parts = halves(hidden)
    width_parts = halves(own_x.shape[1])

    x_pieces = [own_x] + [from_xor(own_x, k) for k in range(1, cols)]
    silu, slope = gates(place, gate, row_count)
    late_g, silu, slope = lax.optimization_barrier((own_g, silu, slope))
    g_pieces = [own_g] + [from_xor(late_g, k) for k in range(1, cols)]

    def rounds(pieces, first_weight, second_weight, residual, weight_rows, step, name):
        part0, tokens = first_product(place, pieces, first_weight, hidden_parts[0], weight_rows, name + "_a")
        mine, theirs = [part0], [other_row(part0)]
        for part in hidden_parts[1:]:
            mine.append(first_product(place, tokens, first_weight, part, weight_rows, name + "_b"))
            theirs.append(other_row(mine[-1]))
        values = blend(silu, mine, theirs, hidden_parts, name + "_blend")
        arrived = []
        for part in width_parts:
            blocks = second_product(place, values, second_weight, residual, part, weight_rows, cols, name + "_out")
            arrived.append([to_block(block, k, step) for k, block in enumerate(blocks)])
        return mine, theirs, arrived

    up_mine, up_theirs, forward = rounds(x_pieces, up_weight, down_weight, own_x, False, 1, "fore")
    back_mine, back_theirs, backward = rounds(g_pieces, down_weight, up_weight, own_g, True, -1, "back")
    gate_grad = gate_gradient(place, slope, up_mine, up_theirs, back_mine, back_theirs, hidden_parts)
    handed_forward = collect(forward, "fore_collect")
    handed_back = collect(backward, "back_collect")
    return handed_forward[None], gate_grad[None], handed_back[None]


def solution(mesh):
    placed = (
        P("section", "col", "row"),
        P("section", None, "col"),
        P("row", "col"),
        P("col", "row"),
        P("section", "col", "row"),
    )
    sizes = mesh.shape
    return jax.shard_map(
        functools.partial(shards, sizes["section"], sizes["col"], sizes["row"]),
        mesh=mesh,
        in_specs=placed,
        out_specs=(
            P("section", "col", "row"),
            P("section", "row", "col"),
            P("section", "col", "row"),
        ),
        check_vma=False,
    )
```

```python
import functools

import jax
import jax.numpy as jnp
from jax import lax
from jax.experimental import pallas as pl
from jax.experimental.pallas import tpu as pltpu
from jax.sharding import PartitionSpec as P

MIB = 1 << 20
COST = {"fore_first_0": 20_000_000_000, "back_second": 20_000_000_000, "prepare": 80_000_000_000}
VMEM = pl.BlockSpec(memory_space=pltpu.VMEM)
SMEM = pl.BlockSpec(memory_space=pltpu.SMEM)
ANY = pl.BlockSpec(memory_space=pl.ANY)
F32 = jnp.float32
BF16 = jnp.bfloat16


def spans(extent, width):
    return [(start, min(width, extent - start)) for start in range(0, extent, width)]


def halves(extent):
    first = -(-extent // 256) * 128
    return [(0, first), (first, extent - first)]


def shape(dims, dtype):
    return jax.ShapeDtypeStruct(tuple(dims), dtype)


def in_vmem(dims, dtype):
    return pltpu.VMEM(tuple(dims), dtype)


def from_hbm(value):
    return pltpu.with_memory_space_constraint(value, pltpu.HBM)


def kernel_call(body, name, outs, args, scratch=(), limit=8 * MIB, smem=0, far=0, aliases={}):
    return pl.pallas_call(
        body,
        name=name,
        out_shape=outs,
        in_specs=[SMEM] * smem + [VMEM] * (len(args) - smem - far) + [ANY] * far,
        out_specs=[VMEM] * len(outs),
        scratch_shapes=list(scratch),
        input_output_aliases=aliases,
        compiler_params=pltpu.CompilerParams(vmem_limit_bytes=limit),
        cost_estimate=pl.CostEstimate(flops=COST.get(name, 0), bytes_accessed=0, transcendentals=0),
    )(*args)


def row_copies(source, target, sems, cuts):
    deep = target.shape[0] // cuts
    return [
        pltpu.make_async_copy(
            source.at[pl.ds(c * deep, deep), :], target.at[pl.ds(c * deep, deep), :], sems.at[c]
        )
        for c in range(cuts)
    ]


def prepare(place, gate, weights, row_count):
    tokens, hidden = gate.shape
    own = tokens // row_count
    cuts = 4

    def body(place_ref, gate_hbm, *refs):
        weight_hbms, (silu_ref, slope_ref), refs = refs[:2], refs[2:4], refs[4:]
        weight_refs, (gate_ref, gate_sem, sems) = refs[:2], refs[2:]
        gate_copy = pltpu.make_async_copy(gate_hbm, gate_ref, gate_sem)
        gate_copy.start()
        copies = []
        for k in range(2):
            copies += row_copies(weight_hbms[k], weight_refs[k], sems.at[k], cuts)
        for copy in copies:
            copy.start()
        gate_copy.wait()
        start = pl.multiple_of(place_ref[1] * own, own)
        for at, wide in spans(hidden, 512):
            value = gate_ref[:, at : at + wide].astype(F32)
            sig = 1.0 / (1.0 + jnp.exp(-value))
            silu_ref[:, at : at + wide] = value * sig
            value = gate_ref[pl.ds(start, own), at : at + wide].astype(F32)
            sig = 1.0 / (1.0 + jnp.exp(-value))
            slope_ref[:, at : at + wide] = sig * (1.0 + value * (1.0 - sig))
        for copy in copies:
            copy.wait()

    return kernel_call(
        body,
        "prepare",
        [shape((tokens, hidden), F32), shape((own, hidden), F32)] + [in_vmem(w.shape, w.dtype) for w in weights],
        [place, from_hbm(gate)] + [from_hbm(w) for w in weights],
        scratch=[pltpu.VMEM(gate.shape, gate.dtype), pltpu.SemaphoreType.DMA, pltpu.SemaphoreType.DMA((2, cuts))],
        smem=1,
        far=3,
    )


def relay(value, after, name):
    def body(*refs):
        pass

    return kernel_call(
        body, name, [shape(value.shape, value.dtype)], [value] + list(after), far=len(after), aliases={0: 0}
    )[0]


def first_product(place, pieces, tokens, weight, part, transposed, name, keep=(), after=()):
    at0, wide0 = part
    fresh = tokens is None
    count = len(pieces) if fresh else 0
    inner = weight.shape[1] if transposed else weight.shape[0]
    rows = pieces[0].shape[0]
    total = rows * len(pieces)
    direct = rows % 16 == 0

    def body(place_ref, *refs):
        refs = list(refs)
        piece_refs = [refs.pop(0) for _ in range(count)]
        held_ref = None if fresh else refs.pop(0)
        weight_ref = refs.pop(0)
        del refs[: len(keep) + len(after)]
        out_ref = refs.pop(0)
        if fresh:
            held_ref = refs.pop(0)
            wide_ref = held_ref if direct else refs.pop(0)
            for k, piece_ref in enumerate(piece_refs):
                at = pl.multiple_of(lax.bitwise_xor(place_ref[0], k) * rows, rows)
                wide_ref[pl.ds(at, rows), :] = piece_ref[...].astype(wide_ref.dtype)
            if not direct:
                held_ref[...] = wide_ref[...].astype(BF16)
        for at, wide in spans(wide0, 512):
            cut = slice(at0 + at, at0 + at + wide)
            if transposed:
                value = lax.dot_general(
                    weight_ref[cut, :], held_ref[...], (((1,), (1,)), ((), ())), preferred_element_type=F32
                ).T
            else:
                value = jnp.dot(held_ref[...], weight_ref[:, cut], preferred_element_type=F32)
            out_ref[:, at : at + wide] = value

    outs = [shape((total, wide0), F32)]
    scratch = []
    if fresh:
        outs.append(shape((total, inner), BF16))
        if not direct:
            scratch.append(pltpu.VMEM((total, inner), F32))
    return kernel_call(
        body,
        name,
        outs,
        [place] + (pieces if fresh else [tokens]) + [weight] + list(keep) + list(after),
        scratch=scratch,
        smem=1,
        far=len(after),
    )


def blend(silu_ref, sum_refs, parts, values_ref):
    for (at0, wide0), (mine_ref, theirs_ref) in zip(parts, sum_refs):
        for at, wide in spans(wide0, 256):
            total = mine_ref[:, at : at + wide] + theirs_ref[:, at : at + wide]
            whole = slice(at0 + at, at0 + at + wide)
            values_ref[:, whole] = (silu_ref[:, whole] * total).astype(BF16)


def second_product(place, silu, sums, parts, residual, weight, transposed, blocks, paired, name, keep=(), after=()):
    tokens, hidden = silu.shape
    width = residual.shape[1]
    rows = tokens // blocks
    flat = [a for pair in sums for a in pair]
    odd = blocks // 2

    def body(place_ref, silu_ref, residual_ref, *refs):
        refs = list(refs)
        sum_refs = [(refs.pop(0), refs.pop(0)) for _ in parts]
        weight_ref = refs.pop(0)
        del refs[: len(keep) + len(after)]
        outs = [refs.pop(0) for _ in range(2 if paired else blocks)]
        values_ref, total_ref = refs
        blend(silu_ref, sum_refs, parts, values_ref)
        for at, wide in spans(width, 512):
            cut = slice(at, at + wide)
            if transposed:
                value = lax.dot_general(
                    weight_ref[cut, :], values_ref[...], (((1,), (1,)), ((), ())), preferred_element_type=F32
                ).T
            else:
                value = jnp.dot(values_ref[...], weight_ref[:, cut], preferred_element_type=F32)
            total_ref[:, cut] = value
            for k in range(blocks):
                start = pl.multiple_of(lax.bitwise_xor(place_ref[0], k) * rows, rows)
                piece = total_ref[pl.ds(start, rows), cut]
                if k == 0:
                    piece = piece + residual_ref[:, cut].astype(F32)
                if paired:
                    low = k // 2 * rows
                    outs[1 - k % 2][low : low + rows, cut] = piece.astype(outs[1 - k % 2].dtype)
                else:
                    outs[k][:, cut] = piece.astype(BF16)

    if paired:
        outs = [shape((odd * rows, width), BF16), shape((odd * rows, width), F32)]
    else:
        outs = [shape((rows, width), BF16)] * blocks
    return kernel_call(
        body,
        name,
        outs,
        [place, silu, residual] + flat + [weight] + list(keep) + list(after),
        scratch=[pltpu.VMEM((tokens, hidden), BF16), pltpu.VMEM((tokens, width), F32)],
        smem=1,
        far=len(after),
    )


def pair_sums(mine, theirs, count, name, after=()):
    rows = mine.shape[0] // count

    def body(mine_ref, theirs_ref, *refs):
        outs = refs[len(after) :]
        for k in range(count):
            low = slice(k * rows, (k + 1) * rows)
            outs[k][...] = (mine_ref[low, :] + theirs_ref[low, :].astype(F32)).astype(BF16)

    return kernel_call(
        body,
        name,
        [shape((rows, mine.shape[1]), BF16)] * count,
        [mine, theirs] + list(after),
        far=len(after),
    )


def gate_gradient(place, slope, up_sums, up_parts, back_sums, back_parts):
    own, hidden = slope.shape

    def body(place_ref, slope_ref, *refs):
        refs = list(refs)
        up_refs = [(refs.pop(0), refs.pop(0)) for _ in up_parts]
        back_refs = [(refs.pop(0), refs.pop(0)) for _ in back_parts]
        out_ref = refs[0]
        rows = pl.ds(pl.multiple_of(place_ref[1] * own, own), own)

        def total(pairs, parts, at):
            for (mine_ref, theirs_ref), (low, wide) in zip(pairs, parts):
                if low <= at < low + wide:
                    cut = slice(at - low, at - low + 128)
                    return mine_ref[rows, cut] + theirs_ref[rows, cut]

        for at in range(0, hidden, 128):
            up = total(up_refs, up_parts, at)
            back = total(back_refs, back_parts, at)
            out_ref[:, at : at + 128] = (back * up * slope_ref[:, at : at + 128]).astype(BF16)

    return kernel_call(
        body,
        "gate_gradient",
        [shape((own, hidden), BF16)],
        [place, slope] + [a for pair in up_sums for a in pair] + [a for pair in back_sums for a in pair],
        smem=1,
    )[0]


def collect(pieces, name):
    def body(*refs):
        out_ref = refs[-1]
        total = refs[0][...].astype(F32)
        for ref in refs[1:-1]:
            total = total + ref[...].astype(F32)
        out_ref[...] = total.astype(BF16)

    return kernel_call(body, name, [shape(pieces[0].shape, BF16)], pieces)[0]


def shards(sections, cols, row_count, inputs, gate_pre, up_weight, down_weight, output_grad):
    own_x, own_g, gate = inputs[0], output_grad[0], gate_pre[0]
    place = jnp.stack([lax.axis_index("col"), lax.axis_index("row")]).astype(jnp.int32)

    def from_xor(value, k):
        return lax.ppermute(value, "col", [(c, c ^ k) for c in range(cols)])

    def to_block(value, k, step):
        pairs = [
            (s * cols + c, (s + step) % sections * cols + (c ^ k)) for s in range(sections) for c in range(cols)
        ]
        return lax.ppermute(value, ("section", "col"), pairs)

    def other_row(value):
        return lax.ppermute(value, "row", [(r, (r + 1) % row_count) for r in range(row_count)])

    hidden = gate.shape[1]
    parts = halves(hidden)
    whole = [(0, hidden)]

    def first_pieces(own):
        pieces = [own] + [None] * (cols - 1)
        for k in list(range(2, cols, 2)) + [1]:
            pieces[k] = from_xor(own, k)
        return pieces

    def last_pieces(pieces, after, name):
        for k in range(3, cols, 2):
            pieces[k] = from_xor(relay(pieces[k - 1], after, name), 1)

    g_pieces, x_pieces = first_pieces(own_g), first_pieces(own_x)
    silu, slope, down, up = prepare(place, gate, [down_weight, up_weight], row_count)
    last_pieces(g_pieces, [silu], "relay_g")
    last_pieces(x_pieces, [silu], "relay_x")

    def sums_of(pieces, weight, transposed, cuts, name, keep, after=()):
        sums, tokens = [], None
        for part in cuts:
            got = first_product(
                place, pieces, tokens, weight, part, transposed, name + "_%d" % len(sums), keep, after
            )
            sums.append((got[0], other_row(got[0])))
            tokens = got[1] if tokens is None else tokens
            after = ()
        return sums

    def reduced(silu_sums, cuts, residual, weight, transposed, paired, step, name, keep, after):
        blocks = second_product(
            place, silu, silu_sums, cuts, residual, weight, transposed, cols, paired, name, keep, after
        )
        if not paired:
            return blocks[0], lambda after: [to_block(block, k, step) for k, block in enumerate(blocks)]
        theirs = from_xor(blocks[0], 1)

        def finish(after):
            halves_ = pair_sums(blocks[1], theirs, cols // 2, name + "_pair", after)
            return [to_block(block, 2 * k, step) for k, block in reversed(list(enumerate(halves_)))]

        return blocks[0], finish

    back_sums = sums_of(g_pieces, down, True, parts, "back_first", [up])
    up_sums = sums_of(x_pieces, up, False, whole, "fore_first", [down], [back_sums[-1][0]])
    token, finish_back = reduced(
        back_sums, parts, own_g, up, True, True, -1, "back_second", [down], [up_sums[-1][0]]
    )
    token, finish_fore = reduced(up_sums, whole, own_x, down, False, True, 1, "fore_second", [], [token])
    backward = finish_back([token])
    forward = finish_fore([])

    gate_grad = gate_gradient(place, slope, up_sums, whole, back_sums, parts)
    handed_back = collect(backward, "back_collect")
    handed_forward = collect(forward, "fore_collect")
    return handed_forward[None], gate_grad[None], handed_back[None]


def solution(mesh):
    placed = (
        P("section", "col", "row"),
        P("section", None, "col"),
        P("row", "col"),
        P("col", "row"),
        P("section", "col", "row"),
    )
    sizes = mesh.shape
    return jax.shard_map(
        functools.partial(shards, sizes["section"], sizes["col"], sizes["row"]),
        mesh=mesh,
        in_specs=placed,
        out_specs=(
            P("section", "col", "row"),
            P("section", "row", "col"),
            P("section", "col", "row"),
        ),
        check_vma=False,
    )
```

```python
import functools

import jax
import jax.numpy as jnp
from jax import lax
from jax.experimental import pallas as pl
from jax.experimental.pallas import tpu as pltpu
from jax.sharding import PartitionSpec as P

MIB = 1 << 20
COST = {'prepare': 5000000000, 'back_first_0': 5000000000, 'back_second': 5000000000, 'fore_second': 5000000000}
VMEM = pl.BlockSpec(memory_space=pltpu.VMEM)
SMEM = pl.BlockSpec(memory_space=pltpu.SMEM)
ANY = pl.BlockSpec(memory_space=pl.ANY)
F32 = jnp.float32
BF16 = jnp.bfloat16


def spans(extent, width):
    return [(start, min(width, extent - start)) for start in range(0, extent, width)]


def shape(dims, dtype):
    return jax.ShapeDtypeStruct(tuple(dims), dtype)


def from_hbm(value):
    return pltpu.with_memory_space_constraint(value, pltpu.HBM)


def kernel_call(body, name, outs, args, scratch=(), limit=8 * MIB, smem=0, far=0):
    return pl.pallas_call(
        body,
        name=name,
        out_shape=outs,
        in_specs=[SMEM] * smem + [VMEM] * (len(args) - smem - far) + [ANY] * far,
        out_specs=[VMEM] * len(outs),
        scratch_shapes=list(scratch),
        compiler_params=pltpu.CompilerParams(vmem_limit_bytes=limit),
        cost_estimate=pl.CostEstimate(flops=COST.get(name, 0), bytes_accessed=0, transcendentals=0),
    )(*args)


def row_copies(source, target, sems, cuts):
    deep = target.shape[0] // cuts
    return [
        pltpu.make_async_copy(
            source.at[pl.ds(c * deep, deep), :], target.at[pl.ds(c * deep, deep), :], sems.at[c]
        )
        for c in range(cuts)
    ]


def prepare(place, gate, row_count, blocks):
    tokens, hidden = gate.shape
    own, rows = tokens // row_count, tokens // blocks
    direct = rows % 16 == 0

    def body(place_ref, gate_hbm, silu_ref, slope_ref, held_ref, sem, *wide):
        copy = pltpu.make_async_copy(gate_hbm, held_ref, sem)
        copy.start()
        copy.wait()
        gate_ref = held_ref if direct else wide[0]
        if not direct:
            gate_ref[...] = held_ref[...].astype(F32)
        start = pl.multiple_of(place_ref[1] * own, own)
        for at, wide in spans(hidden, 512):
            for k in range(blocks):
                from_row = pl.multiple_of(lax.bitwise_xor(place_ref[0], k) * rows, rows)
                value = gate_ref[pl.ds(from_row, rows), at : at + wide].astype(F32)
                silu_ref[k * rows : (k + 1) * rows, at : at + wide] = value / (1.0 + jnp.exp(-value))
            value = gate_ref[pl.ds(start, own), at : at + wide].astype(F32)
            sig = 1.0 / (1.0 + jnp.exp(-value))
            slope_ref[:, at : at + wide] = sig * (1.0 + value * (1.0 - sig))

    return kernel_call(
        body,
        "prepare",
        [shape((tokens, hidden), F32), shape((own, hidden), F32)],
        [place, from_hbm(gate)],
        scratch=[pltpu.VMEM(gate.shape, gate.dtype), pltpu.SemaphoreType.DMA]
        + ([] if direct else [pltpu.VMEM(gate.shape, F32)]),
        smem=1,
        far=1,
    )


def relay(values, after, name):
    count = len(values)

    def body(*refs):
        for k in range(count):
            refs[count + len(after) + k][...] = refs[k][...]

    return kernel_call(body, name, [shape(a.shape, a.dtype) for a in values], [*values, *after], far=len(after))


def first_product(pieces, weight, transposed, part, name, after=()):
    rows, inner = pieces[0].shape
    total = rows * len(pieces)
    base, hidden = part
    direct = rows % 16 == 0
    count = len(pieces)

    def body(*refs):
        piece_refs, weight_ref, (out_ref, *held) = refs[:count], refs[count], refs[count + 1 + len(after) :]
        for k, piece_ref in enumerate(piece_refs):
            held[-1][k * rows : (k + 1) * rows, :] = piece_ref[...].astype(held[-1].dtype)
        if not direct:
            held[0][...] = held[1][...].astype(BF16)
        for at, wide in spans(hidden, 512):
            cut = slice(base + at, base + at + wide)
            if transposed:
                value = lax.dot_general(
                    weight_ref[cut, :], held[0][...], (((1,), (1,)), ((), ())), preferred_element_type=F32
                ).T
            else:
                value = jnp.dot(held[0][...], weight_ref[:, cut], preferred_element_type=F32)
            out_ref[:, at : at + wide] = value

    return kernel_call(
        body,
        name,
        [shape((total, hidden), F32)],
        pieces + [weight] + list(after),
        scratch=[pltpu.VMEM((total, inner), BF16)] + ([] if direct else [pltpu.VMEM((total, inner), F32)]),
        far=len(after),
    )[0]


def second_product(silu, sums, parts, residual, weight, transposed, blocks, name, after=()):
    tokens, hidden = silu.shape
    width = residual.shape[1]
    rows = tokens // blocks
    odd = blocks // 2

    def body(silu_ref, residual_ref, weight_ref, *refs):
        even_out, odd_out, values_ref = refs[-2], refs[-3], refs[-1]
        for k, (base, extent) in enumerate(parts):
            mine_ref, theirs_ref = refs[2 * k], refs[2 * k + 1]
            for at, wide in spans(extent, 256):
                cut, whole = slice(at, at + wide), slice(base + at, base + at + wide)
                values_ref[:, whole] = (silu_ref[:, whole] * (mine_ref[:, cut] + theirs_ref[:, cut])).astype(BF16)
        for at, wide in spans(width, 512):
            cut = slice(at, at + wide)
            if transposed:
                value = lax.dot_general(
                    weight_ref[cut, :], values_ref[...], (((1,), (1,)), ((), ())), preferred_element_type=F32
                ).T
            else:
                value = jnp.dot(values_ref[...], weight_ref[:, cut], preferred_element_type=F32)
            for k in range(blocks):
                piece = value[k * rows : (k + 1) * rows, :]
                if k == 0:
                    piece = piece + residual_ref[:, cut].astype(F32)
                out_ref = odd_out if k % 2 else even_out
                low = k // 2 * rows
                out_ref[low : low + rows, cut] = piece.astype(out_ref.dtype)

    return kernel_call(
        body,
        name,
        [shape((odd * rows, width), BF16), shape((odd * rows, width), F32)],
        [silu, residual, weight] + [a for pair in sums for a in pair] + list(after),
        scratch=[pltpu.VMEM((tokens, hidden), BF16)],
        far=len(after),
    )


def pair_sums(mine, theirs, count, name, after=()):
    rows = mine.shape[0] // count

    def body(mine_ref, theirs_ref, *refs):
        outs = refs[len(after) :]
        for k in range(count):
            low = slice(k * rows, (k + 1) * rows)
            outs[k][...] = (mine_ref[low, :] + theirs_ref[low, :].astype(F32)).astype(BF16)

    return kernel_call(
        body,
        name,
        [shape((rows, mine.shape[1]), BF16)] * count,
        [mine, theirs] + list(after),
        far=len(after),
    )


def gate_gradient(place, slope, up_sums, back_sums, parts, blocks):
    own, hidden = slope.shape
    rows = up_sums[0][0].shape[0] // blocks
    count = own // rows

    def body(place_ref, slope_ref, *refs):
        out_ref = refs[-1]
        for p, (base, extent) in enumerate(parts):
            up_refs, back_refs = refs[2 * p : 2 * p + 2], refs[2 * (len(parts) + p) : 2 * (len(parts) + p) + 2]
            for at, wide in spans(extent, 256):
                cut, whole = slice(at, at + wide), slice(base + at, base + at + wide)
                found = []
                for k in range(count):
                    block = lax.bitwise_xor(place_ref[0], place_ref[1] * count + k)
                    low = pl.ds(pl.multiple_of(block * rows, rows), rows)
                    up = up_refs[0][low, cut] + up_refs[1][low, cut]
                    found.append((back_refs[0][low, cut] + back_refs[1][low, cut]) * up)
                out_ref[:, whole] = (jnp.concatenate(found, axis=0) * slope_ref[:, whole]).astype(BF16)

    return kernel_call(
        body,
        "gate_gradient",
        [shape((own, hidden), BF16)],
        [place, slope] + [a for pair in up_sums + back_sums for a in pair],
        smem=1,
    )[0]


def collect(pieces, name, after=()):
    def body(*refs):
        out_ref, token_ref = refs[-2:]
        total = refs[0][...].astype(F32)
        for ref in refs[1 : len(pieces)]:
            total = total + ref[...].astype(F32)
        out_ref[...] = total.astype(BF16)
        token_ref[...] = jnp.zeros_like(token_ref)

    return kernel_call(
        body,
        name,
        [shape(pieces[0].shape, BF16), shape((8, 128), F32)],
        list(pieces) + list(after),
        far=len(after),
    )


def shards(sections, cols, row_count, inputs, gate_pre, up_weight, down_weight, output_grad):
    own_x, own_g, gate = inputs[0], output_grad[0], gate_pre[0]
    place = jnp.stack([lax.axis_index("col"), lax.axis_index("row")]).astype(jnp.int32)

    def from_xor(value, k):
        return lax.ppermute(value, "col", [(c, c ^ k) for c in range(cols)])

    def to_block(value, k, step):
        pairs = [
            (s * cols + c, (s + step) % sections * cols + (c ^ k)) for s in range(sections) for c in range(cols)
        ]
        return lax.ppermute(value, ("section", "col"), pairs)

    def other_row(value):
        return lax.ppermute(value, "row", [(r, (r + 1) % row_count) for r in range(row_count)])

    even = list(range(2, cols, 2))
    parts = [(0, gate.shape[1])]

    def first_pieces(own):
        return {0: own, **{k: from_xor(own, k) for k in even + [1]}}

    def last_pieces(pieces, after, name):
        for k in even:
            pieces[k + 1] = from_xor(relay([pieces[k]], after, name)[0], 1)
        return [pieces[k] for k in range(cols)]

    def sums_of(pieces, weight, transposed, name, after=()):
        sums = []
        for part in parts:
            mine = first_product(pieces, weight, transposed, part, name + "_%d" % len(sums), after)
            sums.append((mine, other_row(mine)))
            after = [mine]
        return sums

    def finish(mine, theirs, step, name, after):
        blocks = pair_sums(mine, theirs, cols // 2, name, after)
        return blocks[0], [to_block(block, 2 * k, step) for k, block in enumerate(blocks)]

    x_pieces, g_pieces = first_pieces(own_x), first_pieces(own_g)
    silu, slope = prepare(place, gate, row_count, cols)
    x_pieces = last_pieces(x_pieces, [silu, x_pieces[1]], "relay_x")
    g_pieces = last_pieces(g_pieces, [x_pieces[-2]], "relay_g")
    up_sums = sums_of(x_pieces, up_weight, False, "fore_first")
    back_sums = sums_of(g_pieces, down_weight, True, "back_first", [up_sums[-1][0]])
    sent_x, kept_x = second_product(
        silu, up_sums, parts, own_x, down_weight, False, cols, "fore_second", [back_sums[-1][0]]
    )
    other_x = from_xor(sent_x, 1)
    sent_g, kept_g = second_product(silu, back_sums, parts, own_g, up_weight, True, cols, "back_second", [sent_x])
    other_g = from_xor(sent_g, 1)
    token, forward = finish(kept_x, other_x, 1, "fore_pair", [sent_g])
    _, backward = finish(kept_g, other_g, -1, "back_pair", [token])

    gate_grad = gate_gradient(place, slope, up_sums, back_sums, parts, cols)
    handed_forward, token = collect(forward, "fore_collect")
    handed_back, _ = collect(backward, "back_collect", [token])
    return handed_forward[None], gate_grad[None], handed_back[None]


def solution(mesh):
    placed = (
        P("section", "col", "row"),
        P("section", None, "col"),
        P("row", "col"),
        P("col", "row"),
        P("section", "col", "row"),
    )
    sizes = mesh.shape
    return jax.shard_map(
        functools.partial(shards, sizes["section"], sizes["col"], sizes["row"]),
        mesh=mesh,
        in_specs=placed,
        out_specs=(
            P("section", "col", "row"),
            P("section", "row", "col"),
            P("section", "col", "row"),
        ),
        check_vma=False,
    )
```

```python
import functools

import jax
import jax.numpy as jnp
from jax import lax
from jax.experimental import pallas as pl
from jax.experimental.pallas import tpu as pltpu
from jax.sharding import PartitionSpec as P

MIB = 1 << 20
COST = {"prepare": 5_000_000_000, "back_first_0": 5_000_000_000, "back_second": 5_000_000_000, "fore_second": 5_000_000_000}
VMEM = pl.BlockSpec(memory_space=pltpu.VMEM)
SMEM = pl.BlockSpec(memory_space=pltpu.SMEM)
ANY = pl.BlockSpec(memory_space=pl.ANY)
F32 = jnp.float32
BF16 = jnp.bfloat16


def spans(extent, width):
    return [(start, min(width, extent - start)) for start in range(0, extent, width)]


def shape(dims, dtype):
    return jax.ShapeDtypeStruct(tuple(dims), dtype)


def from_hbm(value):
    return pltpu.with_memory_space_constraint(value, pltpu.HBM)


def kernel_call(body, name, outs, args, scratch=(), limit=8 * MIB, smem=0, far=0):
    return pl.pallas_call(
        body,
        name=name,
        out_shape=outs,
        in_specs=[SMEM] * smem + [VMEM] * (len(args) - smem - far) + [ANY] * far,
        out_specs=[VMEM] * len(outs),
        scratch_shapes=list(scratch),
        compiler_params=pltpu.CompilerParams(vmem_limit_bytes=limit),
        cost_estimate=pl.CostEstimate(flops=COST.get(name, 0), bytes_accessed=0, transcendentals=0),
    )(*args)


def prepare(place, gate, row_count, blocks):
    tokens, hidden = gate.shape
    own, rows = tokens // row_count, tokens // blocks
    direct = rows % 16 == 0

    def body(place_ref, gate_hbm, silu_ref, slope_ref, held_ref, sem, *wide):
        copy = pltpu.make_async_copy(gate_hbm, held_ref, sem)
        copy.start()
        copy.wait()
        gate_ref = held_ref if direct else wide[0]
        if not direct:
            gate_ref[...] = held_ref[...].astype(F32)
        start = pl.multiple_of(place_ref[1] * own, own)
        for at, wide in spans(hidden, 512):
            for k in range(blocks):
                from_row = pl.multiple_of(lax.bitwise_xor(place_ref[0], k) * rows, rows)
                value = gate_ref[pl.ds(from_row, rows), at : at + wide].astype(F32)
                silu_ref[k * rows : (k + 1) * rows, at : at + wide] = value / (1.0 + jnp.exp(-value))
            value = gate_ref[pl.ds(start, own), at : at + wide].astype(F32)
            sig = 1.0 / (1.0 + jnp.exp(-value))
            slope_ref[:, at : at + wide] = sig * (1.0 + value * (1.0 - sig))

    return kernel_call(
        body,
        "prepare",
        [shape((tokens, hidden), F32), shape((own, hidden), F32)],
        [place, from_hbm(gate)],
        scratch=[pltpu.VMEM(gate.shape, gate.dtype), pltpu.SemaphoreType.DMA]
        + ([] if direct else [pltpu.VMEM(gate.shape, F32)]),
        smem=1,
        far=1,
    )


def relay(values, after, name):
    count = len(values)

    def body(*refs):
        for k in range(count):
            refs[count + len(after) + k][...] = refs[k][...]

    return kernel_call(body, name, [shape(a.shape, a.dtype) for a in values], [*values, *after], far=len(after))


def first_product(pieces, weight, transposed, part, name, after=()):
    rows, inner = pieces[0].shape
    total = rows * len(pieces)
    base, hidden = part
    direct = rows % 16 == 0
    count = len(pieces)

    def body(*refs):
        piece_refs, weight_ref, (out_ref, *held) = refs[:count], refs[count], refs[count + 1 + len(after) :]
        for k, piece_ref in enumerate(piece_refs):
            held[-1][k * rows : (k + 1) * rows, :] = piece_ref[...].astype(held[-1].dtype)
        if not direct:
            held[0][...] = held[1][...].astype(BF16)
        for at, wide in spans(hidden, 512):
            cut = slice(base + at, base + at + wide)
            if transposed:
                value = lax.dot_general(
                    weight_ref[cut, :], held[0][...], (((1,), (1,)), ((), ())), preferred_element_type=F32
                ).T
            else:
                value = jnp.dot(held[0][...], weight_ref[:, cut], preferred_element_type=F32)
            out_ref[:, at : at + wide] = value

    return kernel_call(
        body,
        name,
        [shape((total, hidden), F32)],
        pieces + [weight] + list(after),
        scratch=[pltpu.VMEM((total, inner), BF16)] + ([] if direct else [pltpu.VMEM((total, inner), F32)]),
        far=len(after),
    )[0]


def second_product(silu, sums, parts, residual, weight, transposed, blocks, groups, name, after=()):
    tokens, hidden = silu.shape
    width = residual.shape[1]
    rows = tokens // blocks
    odd = blocks // 2

    def body(silu_ref, residual_ref, weight_ref, *refs):
        odd_outs, even_out, values_ref = refs[-2 - len(groups) : -2], refs[-2], refs[-1]
        for k, (base, extent) in enumerate(parts):
            mine_ref, theirs_ref = refs[2 * k], refs[2 * k + 1]
            for at, wide in spans(extent, 256):
                cut, whole = slice(at, at + wide), slice(base + at, base + at + wide)
                values_ref[:, whole] = (silu_ref[:, whole] * (mine_ref[:, cut] + theirs_ref[:, cut])).astype(BF16)
        for at, wide in spans(width, 512):
            cut = slice(at, at + wide)
            if transposed:
                value = lax.dot_general(
                    weight_ref[cut, :], values_ref[...], (((1,), (1,)), ((), ())), preferred_element_type=F32
                ).T
            else:
                value = jnp.dot(values_ref[...], weight_ref[:, cut], preferred_element_type=F32)
            for k in range(blocks):
                piece = value[k * rows : (k + 1) * rows, :]
                if k == 0:
                    piece = piece + residual_ref[:, cut].astype(F32)
                out_ref, low = even_out, k // 2 * rows
                if k % 2:
                    out_ref, low = next(
                        (ref, group.index(k // 2) * rows) for ref, group in zip(odd_outs, groups) if k // 2 in group
                    )
                out_ref[low : low + rows, cut] = piece.astype(out_ref.dtype)

    return kernel_call(
        body,
        name,
        [shape((len(group) * rows, width), BF16) for group in groups] + [shape((odd * rows, width), F32)],
        [silu, residual, weight] + [a for pair in sums for a in pair] + list(after),
        scratch=[pltpu.VMEM((tokens, hidden), BF16)],
        far=len(after),
    )


def pair_sums(mine, theirs, group, count, name, after=()):
    rows = mine.shape[0] // count

    def body(mine_ref, theirs_ref, *refs):
        outs = refs[len(after) :]
        for k, j in enumerate(group):
            near, far = slice(j * rows, (j + 1) * rows), slice(k * rows, (k + 1) * rows)
            outs[k][...] = (mine_ref[near, :] + theirs_ref[far, :].astype(F32)).astype(BF16)

    return kernel_call(
        body,
        name,
        [shape((rows, mine.shape[1]), BF16)] * len(group),
        [mine, theirs] + list(after),
        far=len(after),
    )


def gate_gradient(place, slope, up_sums, back_sums, parts, blocks):
    own, hidden = slope.shape
    rows = up_sums[0][0].shape[0] // blocks
    count = own // rows

    def body(place_ref, slope_ref, *refs):
        out_ref = refs[-1]
        for p, (base, extent) in enumerate(parts):
            up_refs, back_refs = refs[2 * p : 2 * p + 2], refs[2 * (len(parts) + p) : 2 * (len(parts) + p) + 2]
            for at, wide in spans(extent, 256):
                cut, whole = slice(at, at + wide), slice(base + at, base + at + wide)
                found = []
                for k in range(count):
                    block = lax.bitwise_xor(place_ref[0], place_ref[1] * count + k)
                    low = pl.ds(pl.multiple_of(block * rows, rows), rows)
                    up = up_refs[0][low, cut] + up_refs[1][low, cut]
                    found.append((back_refs[0][low, cut] + back_refs[1][low, cut]) * up)
                out_ref[:, whole] = (jnp.concatenate(found, axis=0) * slope_ref[:, whole]).astype(BF16)

    return kernel_call(
        body,
        "gate_gradient",
        [shape((own, hidden), BF16)],
        [place, slope] + [a for pair in up_sums + back_sums for a in pair],
        smem=1,
    )[0]


def collect(pieces, name, after=()):
    def body(*refs):
        out_ref, token_ref = refs[-2:]
        total = refs[0][...].astype(F32)
        for ref in refs[1 : len(pieces)]:
            total = total + ref[...].astype(F32)
        out_ref[...] = total.astype(BF16)
        token_ref[...] = jnp.zeros_like(token_ref)

    return kernel_call(
        body,
        name,
        [shape(pieces[0].shape, BF16), shape((8, 128), F32)],
        list(pieces) + list(after),
        far=len(after),
    )


def shards(sections, cols, row_count, inputs, gate_pre, up_weight, down_weight, output_grad):
    own_x, own_g, gate = inputs[0], output_grad[0], gate_pre[0]
    place = jnp.stack([lax.axis_index("col"), lax.axis_index("row")]).astype(jnp.int32)

    def from_xor(value, k):
        return lax.ppermute(value, "col", [(c, c ^ k) for c in range(cols)])

    def to_block(value, k, step):
        pairs = [
            (s * cols + c, (s + step) % sections * cols + (c ^ k)) for s in range(sections) for c in range(cols)
        ]
        return lax.ppermute(value, ("section", "col"), pairs)

    def other_row(value):
        return lax.ppermute(value, "row", [(r, (r + 1) % row_count) for r in range(row_count)])

    even = list(range(2, cols, 2))
    parts = [(0, gate.shape[1])]

    def first_pieces(own):
        return {0: own, **{k: from_xor(own, k) for k in even + [1]}}

    def last_pieces(pieces, after, name):
        for k in even:
            pieces[k + 1] = from_xor(relay([pieces[k]], after, name)[0], 1)
        return [pieces[k] for k in range(cols)]

    def sums_of(pieces, weight, transposed, name, after=()):
        sums = []
        for part in parts:
            mine = first_product(pieces, weight, transposed, part, name + "_%d" % len(sums), after)
            sums.append((mine, other_row(mine)))
            after = [mine]
        return sums

    def finish(mine, theirs, groups, step, name, after):
        arrived = []
        for array, group in zip(theirs, groups):
            blocks = pair_sums(mine, array, group, cols // 2, name + "_%d" % len(arrived), after)
            arrived += [to_block(block, 2 * j, step) for j, block in zip(group, blocks)]
            after = [blocks[0]]
        return after[0], arrived

    x_pieces, g_pieces = first_pieces(own_x), first_pieces(own_g)
    silu, slope = prepare(place, gate, row_count, cols)
    x_pieces = last_pieces(x_pieces, [silu, x_pieces[1]], "relay_x")
    g_pieces = last_pieces(g_pieces, [x_pieces[-2]], "relay_g")
    up_sums = sums_of(x_pieces, up_weight, False, "fore_first")
    back_sums = sums_of(g_pieces, down_weight, True, "back_first", [up_sums[-1][0]])
    groups = [list(range(1, cols // 2)), [0]]
    *sent_x, kept_x = second_product(
        silu, up_sums, parts, own_x, down_weight, False, cols, groups, "fore_second", [back_sums[-1][0]]
    )
    other_x = [from_xor(sent, 1) for sent in sent_x]
    *sent_g, kept_g = second_product(
        silu, back_sums, parts, own_g, up_weight, True, cols, groups, "back_second", sent_x[:1]
    )
    other_g = [from_xor(sent, 1) for sent in sent_g]
    token, forward = finish(kept_x, other_x, groups, 1, "fore_pair", sent_g[:1])
    _, backward = finish(kept_g, other_g, groups, -1, "back_pair", [token])

    gate_grad = gate_gradient(place, slope, up_sums, back_sums, parts, cols)
    handed_forward, token = collect(forward, "fore_collect")
    handed_back, _ = collect(backward, "back_collect", [token])
    return handed_forward[None], gate_grad[None], handed_back[None]


def solution(mesh):
    placed = (
        P("section", "col", "row"),
        P("section", None, "col"),
        P("row", "col"),
        P("col", "row"),
        P("section", "col", "row"),
    )
    sizes = mesh.shape
    return jax.shard_map(
        functools.partial(shards, sizes["section"], sizes["col"], sizes["row"]),
        mesh=mesh,
        in_specs=placed,
        out_specs=(
            P("section", "col", "row"),
            P("section", "row", "col"),
            P("section", "col", "row"),
        ),
        check_vma=False,
    )
```

```python
import functools

import jax
import jax.numpy as jnp
from jax import lax
from jax.experimental import pallas as pl
from jax.experimental.pallas import tpu as pltpu
from jax.sharding import PartitionSpec as P

MIB = 1 << 20
COST = dict.fromkeys(("prepare", "back_first_0", "back_second", "fore_second", "mark"), 5_000_000_000)
VMEM = pl.BlockSpec(memory_space=pltpu.VMEM)
SMEM = pl.BlockSpec(memory_space=pltpu.SMEM)
ANY = pl.BlockSpec(memory_space=pl.ANY)
F32 = jnp.float32
BF16 = jnp.bfloat16


def spans(extent, width):
    return [(start, min(width, extent - start)) for start in range(0, extent, width)]


def shape(dims, dtype):
    return jax.ShapeDtypeStruct(tuple(dims), dtype)


def from_hbm(value):
    return pltpu.with_memory_space_constraint(value, pltpu.HBM)


def kernel_call(body, name, outs, args, scratch=(), limit=8 * MIB, smem=0, far=0):
    return pl.pallas_call(
        body,
        name=name,
        out_shape=outs,
        in_specs=[SMEM] * smem + [VMEM] * (len(args) - smem - far) + [ANY] * far,
        out_specs=[VMEM] * len(outs),
        scratch_shapes=list(scratch),
        compiler_params=pltpu.CompilerParams(vmem_limit_bytes=limit),
        cost_estimate=pl.CostEstimate(flops=COST.get(name, 0), bytes_accessed=0, transcendentals=0),
    )(*args)


def prepare(place, gate, row_count, blocks):
    tokens, hidden = gate.shape
    own, rows = tokens // row_count, tokens // blocks
    direct = rows % 16 == 0

    def body(place_ref, gate_hbm, silu_ref, slope_ref, held_ref, sem, *wide):
        copy = pltpu.make_async_copy(gate_hbm, held_ref, sem)
        copy.start()
        copy.wait()
        gate_ref = held_ref if direct else wide[0]
        if not direct:
            gate_ref[...] = held_ref[...].astype(F32)
        start = pl.multiple_of(place_ref[1] * own, own)
        for at, wide in spans(hidden, 512):
            for k in range(blocks):
                from_row = pl.multiple_of(lax.bitwise_xor(place_ref[0], k) * rows, rows)
                value = gate_ref[pl.ds(from_row, rows), at : at + wide].astype(F32)
                silu_ref[k * rows : (k + 1) * rows, at : at + wide] = value / (1.0 + jnp.exp(-value))
            value = gate_ref[pl.ds(start, own), at : at + wide].astype(F32)
            sig = 1.0 / (1.0 + jnp.exp(-value))
            slope_ref[:, at : at + wide] = sig * (1.0 + value * (1.0 - sig))

    return kernel_call(
        body,
        "prepare",
        [shape((tokens, hidden), F32), shape((own, hidden), F32)],
        [place, from_hbm(gate)],
        scratch=[pltpu.VMEM(gate.shape, gate.dtype), pltpu.SemaphoreType.DMA]
        + ([] if direct else [pltpu.VMEM(gate.shape, F32)]),
        smem=1,
        far=1,
    )


def relay(values, after, name):
    count = len(values)

    def body(*refs):
        for k in range(count):
            refs[count + len(after) + k][...] = refs[k][...]

    return kernel_call(body, name, [shape(a.shape, a.dtype) for a in values], [*values, *after], far=len(after))


def first_product(pieces, weight, transposed, part, name, after=()):
    rows, inner = pieces[0].shape
    total = rows * len(pieces)
    base, hidden = part
    direct = rows % 16 == 0
    count = len(pieces)

    def body(*refs):
        piece_refs, weight_ref, (out_ref, *held) = refs[:count], refs[count], refs[count + 1 + len(after) :]
        for k, piece_ref in enumerate(piece_refs):
            held[-1][k * rows : (k + 1) * rows, :] = piece_ref[...].astype(held[-1].dtype)
        if not direct:
            held[0][...] = held[1][...].astype(BF16)
        for at, wide in spans(hidden, 512):
            cut = slice(base + at, base + at + wide)
            if transposed:
                value = lax.dot_general(
                    weight_ref[cut, :], held[0][...], (((1,), (1,)), ((), ())), preferred_element_type=F32
                ).T
            else:
                value = jnp.dot(held[0][...], weight_ref[:, cut], preferred_element_type=F32)
            out_ref[:, at : at + wide] = value

    return kernel_call(
        body,
        name,
        [shape((total, hidden), F32)],
        pieces + [weight] + list(after),
        scratch=[pltpu.VMEM((total, inner), BF16)] + ([] if direct else [pltpu.VMEM((total, inner), F32)]),
        far=len(after),
    )[0]


def second_product(silu, sums, parts, residual, weight, transposed, blocks, groups, name, after=()):
    tokens, hidden = silu.shape
    width = residual.shape[1]
    rows = tokens // blocks
    odd = blocks // 2

    def body(silu_ref, residual_ref, weight_ref, *refs):
        odd_outs, even_out, values_ref = refs[-2 - len(groups) : -2], refs[-2], refs[-1]
        for k, (base, extent) in enumerate(parts):
            mine_ref, theirs_ref = refs[2 * k], refs[2 * k + 1]
            for at, wide in spans(extent, 256):
                cut, whole = slice(at, at + wide), slice(base + at, base + at + wide)
                values_ref[:, whole] = (silu_ref[:, whole] * (mine_ref[:, cut] + theirs_ref[:, cut])).astype(BF16)
        for at, wide in spans(width, 512):
            cut = slice(at, at + wide)
            if transposed:
                value = lax.dot_general(
                    weight_ref[cut, :], values_ref[...], (((1,), (1,)), ((), ())), preferred_element_type=F32
                ).T
            else:
                value = jnp.dot(values_ref[...], weight_ref[:, cut], preferred_element_type=F32)
            for k in range(blocks):
                piece = value[k * rows : (k + 1) * rows, :]
                if k == 0:
                    piece = piece + residual_ref[:, cut].astype(F32)
                out_ref, low = even_out, k // 2 * rows
                if k % 2:
                    out_ref, low = next(
                        (ref, group.index(k // 2) * rows) for ref, group in zip(odd_outs, groups) if k // 2 in group
                    )
                out_ref[low : low + rows, cut] = piece.astype(out_ref.dtype)

    return kernel_call(
        body,
        name,
        [shape((len(group) * rows, width), BF16) for group in groups] + [shape((odd * rows, width), F32)],
        [silu, residual, weight] + [a for pair in sums for a in pair] + list(after),
        scratch=[pltpu.VMEM((tokens, hidden), BF16)],
        far=len(after),
    )


def pair_sums(mine, theirs, group, count, name, after=()):
    rows = mine.shape[0] // count

    def body(mine_ref, theirs_ref, *refs):
        outs = refs[len(after) :]
        for k, j in enumerate(group):
            near, far = slice(j * rows, (j + 1) * rows), slice(k * rows, (k + 1) * rows)
            outs[k][...] = (mine_ref[near, :] + theirs_ref[far, :].astype(F32)).astype(BF16)

    return kernel_call(
        body,
        name,
        [shape((rows, mine.shape[1]), BF16)] * len(group),
        [mine, theirs] + list(after),
        far=len(after),
    )


def gate_gradient(place, slope, up_sums, back_sums, parts, blocks):
    own, hidden = slope.shape
    rows = up_sums[0][0].shape[0] // blocks
    count = own // rows

    def body(place_ref, slope_ref, *refs):
        out_ref = refs[-1]
        for p, (base, extent) in enumerate(parts):
            up_refs, back_refs = refs[2 * p : 2 * p + 2], refs[2 * (len(parts) + p) : 2 * (len(parts) + p) + 2]
            for at, wide in spans(extent, 256):
                cut, whole = slice(at, at + wide), slice(base + at, base + at + wide)
                found = []
                for k in range(count):
                    block = lax.bitwise_xor(place_ref[0], place_ref[1] * count + k)
                    low = pl.ds(pl.multiple_of(block * rows, rows), rows)
                    up = up_refs[0][low, cut] + up_refs[1][low, cut]
                    found.append((back_refs[0][low, cut] + back_refs[1][low, cut]) * up)
                out_ref[:, whole] = (jnp.concatenate(found, axis=0) * slope_ref[:, whole]).astype(BF16)

    return kernel_call(
        body,
        "gate_gradient",
        [shape((own, hidden), BF16)],
        [place, slope] + [a for pair in up_sums + back_sums for a in pair],
        smem=1,
    )[0]


def collect(pieces, name, after=()):
    def body(*refs):
        out_ref, token_ref = refs[-2:]
        total = refs[0][...].astype(F32)
        for ref in refs[1 : len(pieces)]:
            total = total + ref[...].astype(F32)
        out_ref[...] = total.astype(BF16)
        token_ref[...] = jnp.zeros_like(token_ref)

    return kernel_call(
        body,
        name,
        [shape(pieces[0].shape, BF16), shape((8, 128), F32)],
        list(pieces) + list(after),
        far=len(after),
    )


def shards(sections, cols, row_count, inputs, gate_pre, up_weight, down_weight, output_grad):
    own_x, own_g, gate = inputs[0], output_grad[0], gate_pre[0]
    place = jnp.stack([lax.axis_index("col"), lax.axis_index("row")]).astype(jnp.int32)

    def from_xor(value, k):
        return lax.ppermute(value, "col", [(c, c ^ k) for c in range(cols)])

    def to_block(value, k, step):
        pairs = [
            (s * cols + c, (s + step) % sections * cols + (c ^ k)) for s in range(sections) for c in range(cols)
        ]
        return lax.ppermute(value, ("section", "col"), pairs)

    def other_row(value):
        return lax.ppermute(value, "row", [(r, (r + 1) % row_count) for r in range(row_count)])

    even = list(range(2, cols, 2))
    parts = [(0, gate.shape[1])]

    def first_pieces(own):
        return {0: own, **{k: from_xor(own, k) for k in even + [1]}}

    def last_pieces(pieces, after, name):
        for k in even:
            pieces[k + 1] = from_xor(relay([pieces[k]], after, name)[0], 1)
        return [pieces[k] for k in range(cols)]

    def sums_of(pieces, weight, transposed, name, after=()):
        sums = []
        for part in parts:
            mine = first_product(pieces, weight, transposed, part, name + "_%d" % len(sums), after)
            sums.append((mine, other_row(mine)))
            after = [mine]
        return sums

    def finish(mine, theirs, groups, step, name, after):
        arrived = []
        for array, group in zip(theirs, groups):
            blocks = pair_sums(mine, array, group, cols // 2, name + "_%d" % len(arrived), after)
            arrived += [to_block(block, 2 * j, step) for j, block in zip(group, blocks)]
            after = [blocks[0]]
        return after[0], arrived

    x_pieces, g_pieces = first_pieces(own_x), first_pieces(own_g)
    silu, slope = prepare(place, gate, row_count, cols)
    x_pieces = last_pieces(x_pieces, [silu, x_pieces[1]], "relay_x")
    g_pieces = last_pieces(g_pieces, [x_pieces[-2], g_pieces[1]], "relay_g")
    up_sums = sums_of(x_pieces, up_weight, False, "fore_first")
    back_sums = sums_of(g_pieces, down_weight, True, "back_first", [up_sums[-1][0]])
    x_groups, g_groups = [list(range(cols // 2))], [list(range(1, cols // 2)), [0]]
    *sent_x, kept_x = second_product(
        silu, up_sums, parts, own_x, down_weight, False, cols, x_groups, "fore_second", [back_sums[-1][0]]
    )
    other_x = [from_xor(sent, 1) for sent in sent_x]
    *sent_g, kept_g = second_product(
        silu, back_sums, parts, own_g, up_weight, True, cols, g_groups, "back_second", sent_x[:1]
    )
    other_g = [from_xor(sent, 1) for sent in sent_g]
    token, forward = finish(kept_x, other_x, x_groups, 1, "fore_pair", sent_g[:1])
    _, backward = finish(kept_g, other_g, g_groups, -1, "back_pair", [token])

    gate_grad = gate_gradient(place, slope, up_sums, back_sums, parts, cols)
    handed_forward, token = collect(forward, "fore_collect")
    (token,) = relay([token], backward[:1], "mark")
    handed_back, _ = collect(backward, "back_collect", [token])
    return handed_forward[None], gate_grad[None], handed_back[None]


def solution(mesh):
    placed = (
        P("section", "col", "row"),
        P("section", None, "col"),
        P("row", "col"),
        P("col", "row"),
        P("section", "col", "row"),
    )
    sizes = mesh.shape
    return jax.shard_map(
        functools.partial(shards, sizes["section"], sizes["col"], sizes["row"]),
        mesh=mesh,
        in_specs=placed,
        out_specs=(
            P("section", "col", "row"),
            P("section", "row", "col"),
            P("section", "col", "row"),
        ),
        check_vma=False,
    )
```

```python
import functools

import jax
import jax.numpy as jnp
from jax import lax
from jax.experimental import pallas as pl
from jax.experimental.pallas import tpu as pltpu
from jax.sharding import PartitionSpec as P

MIB = 1 << 20
COST = dict.fromkeys(("prepare", "back_first_0", "back_second", "fore_second", "mark"), 5_000_000_000)
VMEM = pl.BlockSpec(memory_space=pltpu.VMEM)
SMEM = pl.BlockSpec(memory_space=pltpu.SMEM)
ANY = pl.BlockSpec(memory_space=pl.ANY)
F32 = jnp.float32
BF16 = jnp.bfloat16


def spans(extent, width):
    return [(start, min(width, extent - start)) for start in range(0, extent, width)]


def shape(dims, dtype):
    return jax.ShapeDtypeStruct(tuple(dims), dtype)


def from_hbm(value):
    return pltpu.with_memory_space_constraint(value, pltpu.HBM)


def kernel_call(body, name, outs, args, scratch=(), limit=8 * MIB, smem=0, far=0):
    return pl.pallas_call(
        body,
        name=name,
        out_shape=outs,
        in_specs=[SMEM] * smem + [VMEM] * (len(args) - smem - far) + [ANY] * far,
        out_specs=[VMEM] * len(outs),
        scratch_shapes=list(scratch),
        compiler_params=pltpu.CompilerParams(vmem_limit_bytes=limit),
        cost_estimate=pl.CostEstimate(flops=COST.get(name, 0), bytes_accessed=0, transcendentals=0),
    )(*args)


def prepare(place, gate, row_count, blocks):
    tokens, hidden = gate.shape
    own, rows = tokens // row_count, tokens // blocks
    direct = rows % 16 == 0

    def body(place_ref, gate_hbm, silu_ref, slope_ref, held_ref, sem, *wide):
        copy = pltpu.make_async_copy(gate_hbm, held_ref, sem)
        copy.start()
        copy.wait()
        gate_ref = held_ref if direct else wide[0]
        if not direct:
            gate_ref[...] = held_ref[...].astype(F32)
        start = pl.multiple_of(place_ref[1] * own, own)
        for at, wide in spans(hidden, 512):
            for k in range(blocks):
                from_row = pl.multiple_of(lax.bitwise_xor(place_ref[0], k) * rows, rows)
                value = gate_ref[pl.ds(from_row, rows), at : at + wide].astype(F32)
                silu_ref[k * rows : (k + 1) * rows, at : at + wide] = value / (1.0 + jnp.exp(-value))
            value = gate_ref[pl.ds(start, own), at : at + wide].astype(F32)
            sig = 1.0 / (1.0 + jnp.exp(-value))
            slope_ref[:, at : at + wide] = sig * (1.0 + value * (1.0 - sig))

    return kernel_call(
        body,
        "prepare",
        [shape((tokens, hidden), F32), shape((own, hidden), F32)],
        [place, from_hbm(gate)],
        scratch=[pltpu.VMEM(gate.shape, gate.dtype), pltpu.SemaphoreType.DMA]
        + ([] if direct else [pltpu.VMEM(gate.shape, F32)]),
        smem=1,
        far=1,
    )


def relay(values, after, name):
    count = len(values)

    def body(*refs):
        for k in range(count):
            refs[count + len(after) + k][...] = refs[k][...]

    return kernel_call(body, name, [shape(a.shape, a.dtype) for a in values], [*values, *after], far=len(after))


def first_product(pieces, weight, transposed, part, name, after=()):
    rows, inner = pieces[0].shape
    total = rows * len(pieces)
    base, hidden = part
    direct = rows % 16 == 0
    count = len(pieces)

    def body(*refs):
        piece_refs, weight_ref, (out_ref, *held) = refs[:count], refs[count], refs[count + 1 + len(after) :]
        for k, piece_ref in enumerate(piece_refs):
            held[-1][k * rows : (k + 1) * rows, :] = piece_ref[...].astype(held[-1].dtype)
        if not direct:
            held[0][...] = held[1][...].astype(BF16)
        for at, wide in spans(hidden, 512):
            cut = slice(base + at, base + at + wide)
            if transposed:
                value = lax.dot_general(
                    weight_ref[cut, :], held[0][...], (((1,), (1,)), ((), ())), preferred_element_type=F32
                ).T
            else:
                value = jnp.dot(held[0][...], weight_ref[:, cut], preferred_element_type=F32)
            out_ref[:, at : at + wide] = value

    return kernel_call(
        body,
        name,
        [shape((total, hidden), F32)],
        pieces + [weight] + list(after),
        scratch=[pltpu.VMEM((total, inner), BF16)] + ([] if direct else [pltpu.VMEM((total, inner), F32)]),
        far=len(after),
    )[0]


def second_product(silu, sums, parts, residual, weight, transposed, blocks, groups, name, after=()):
    tokens, hidden = silu.shape
    width = residual.shape[1]
    rows = tokens // blocks
    odd = blocks // 2

    def body(silu_ref, residual_ref, weight_ref, *refs):
        odd_outs, even_out, values_ref = refs[-2 - len(groups) : -2], refs[-2], refs[-1]
        for k, (base, extent) in enumerate(parts):
            mine_ref, theirs_ref = refs[2 * k], refs[2 * k + 1]
            for at, wide in spans(extent, 256):
                cut, whole = slice(at, at + wide), slice(base + at, base + at + wide)
                values_ref[:, whole] = (silu_ref[:, whole] * (mine_ref[:, cut] + theirs_ref[:, cut])).astype(BF16)
        for at, wide in spans(width, 512):
            cut = slice(at, at + wide)
            if transposed:
                value = lax.dot_general(
                    weight_ref[cut, :], values_ref[...], (((1,), (1,)), ((), ())), preferred_element_type=F32
                ).T
            else:
                value = jnp.dot(values_ref[...], weight_ref[:, cut], preferred_element_type=F32)
            for k in range(blocks):
                piece = value[k * rows : (k + 1) * rows, :]
                if k == 0:
                    piece = piece + residual_ref[:, cut].astype(F32)
                out_ref, low = even_out, k // 2 * rows
                if k % 2:
                    out_ref, low = next(
                        (ref, group.index(k // 2) * rows) for ref, group in zip(odd_outs, groups) if k // 2 in group
                    )
                out_ref[low : low + rows, cut] = piece.astype(out_ref.dtype)

    return kernel_call(
        body,
        name,
        [shape((len(group) * rows, width), BF16) for group in groups] + [shape((odd * rows, width), F32)],
        [silu, residual, weight] + [a for pair in sums for a in pair] + list(after),
        scratch=[pltpu.VMEM((tokens, hidden), BF16)],
        far=len(after),
    )


def pair_sums(mine, theirs, group, count, name, after=()):
    rows = mine.shape[0] // count

    def body(mine_ref, theirs_ref, *refs):
        outs = refs[len(after) :]
        for k, j in enumerate(group):
            near, far = slice(j * rows, (j + 1) * rows), slice(k * rows, (k + 1) * rows)
            outs[k][...] = (mine_ref[near, :] + theirs_ref[far, :].astype(F32)).astype(BF16)

    return kernel_call(
        body,
        name,
        [shape((rows, mine.shape[1]), BF16)] * len(group),
        [mine, theirs] + list(after),
        far=len(after),
    )


def gate_gradient(place, slope, up_sums, back_sums, parts, blocks, after):
    own, hidden = slope.shape
    rows = up_sums[0][0].shape[0] // blocks
    count = own // rows

    def body(place_ref, slope_ref, *refs):
        out_ref = refs[-1]
        for p, (base, extent) in enumerate(parts):
            up_refs, back_refs = refs[2 * p : 2 * p + 2], refs[2 * (len(parts) + p) : 2 * (len(parts) + p) + 2]
            for at, wide in spans(extent, 256):
                cut, whole = slice(at, at + wide), slice(base + at, base + at + wide)
                found = []
                for k in range(count):
                    block = lax.bitwise_xor(place_ref[0], place_ref[1] * count + k)
                    low = pl.ds(pl.multiple_of(block * rows, rows), rows)
                    up = up_refs[0][low, cut] + up_refs[1][low, cut]
                    found.append((back_refs[0][low, cut] + back_refs[1][low, cut]) * up)
                out_ref[:, whole] = (jnp.concatenate(found, axis=0) * slope_ref[:, whole]).astype(BF16)

    return kernel_call(
        body,
        "gate_gradient",
        [shape((own, hidden), BF16)],
        [place, slope] + [a for pair in up_sums + back_sums for a in pair] + after,
        smem=1,
        far=len(after),
    )[0]


def collect(pieces, name, after=()):
    def body(*refs):
        out_ref, token_ref = refs[-2:]
        total = refs[0][...].astype(F32)
        for ref in refs[1 : len(pieces)]:
            total = total + ref[...].astype(F32)
        out_ref[...] = total.astype(BF16)
        token_ref[...] = jnp.zeros_like(token_ref)

    return kernel_call(
        body,
        name,
        [shape(pieces[0].shape, BF16), shape((8, 128), F32)],
        list(pieces) + list(after),
        far=len(after),
    )


def shards(sections, cols, row_count, inputs, gate_pre, up_weight, down_weight, output_grad):
    own_x, own_g, gate = inputs[0], output_grad[0], gate_pre[0]
    place = jnp.stack([lax.axis_index("col"), lax.axis_index("row")]).astype(jnp.int32)

    def from_xor(value, k):
        return lax.ppermute(value, "col", [(c, c ^ k) for c in range(cols)])

    def to_block(value, k, step):
        pairs = [
            (s * cols + c, (s + step) % sections * cols + (c ^ k)) for s in range(sections) for c in range(cols)
        ]
        return lax.ppermute(value, ("section", "col"), pairs)

    def other_row(value):
        return lax.ppermute(value, "row", [(r, (r + 1) % row_count) for r in range(row_count)])

    even = list(range(2, cols, 2))
    parts = [(0, gate.shape[1])]

    def first_pieces(own):
        return {0: own, **{k: from_xor(own, k) for k in even + [1]}}

    def last_pieces(pieces, after, name):
        for k in even:
            pieces[k + 1] = from_xor(relay([pieces[k]], after, name)[0], 1)
        return [pieces[k] for k in range(cols)]

    def sums_of(pieces, weight, transposed, name, after=()):
        sums = []
        for part in parts:
            mine = first_product(pieces, weight, transposed, part, name + "_%d" % len(sums), after)
            sums.append((mine, other_row(mine)))
            after = [mine]
        return sums

    def finish(mine, theirs, groups, step, name, after):
        arrived = []
        for array, group in zip(theirs, groups):
            blocks = pair_sums(mine, array, group, cols // 2, name + "_%d" % len(arrived), after)
            arrived += [to_block(block, 2 * j, step) for j, block in zip(group, blocks)]
            after = [blocks[0]]
        return after[0], arrived

    x_pieces, g_pieces = first_pieces(own_x), first_pieces(own_g)
    silu, slope = prepare(place, gate, row_count, cols)
    x_pieces = last_pieces(x_pieces, [silu, x_pieces[1]], "relay_x")
    g_pieces = last_pieces(g_pieces, [x_pieces[-2], g_pieces[1]], "relay_g")
    up_sums = sums_of(x_pieces, up_weight, False, "fore_first")
    back_sums = sums_of(g_pieces, down_weight, True, "back_first", [up_sums[-1][0]])
    x_groups, g_groups = [list(range(cols // 2))], [list(range(1, cols // 2)), [0]]
    *sent_x, kept_x = second_product(
        silu, up_sums, parts, own_x, down_weight, False, cols, x_groups, "fore_second", [back_sums[-1][0]]
    )
    other_x = [from_xor(sent, 1) for sent in sent_x]
    *sent_g, kept_g = second_product(
        silu, back_sums, parts, own_g, up_weight, True, cols, g_groups, "back_second", sent_x[:1]
    )
    other_g = [from_xor(sent, 1) for sent in sent_g]
    token, forward = finish(kept_x, other_x, x_groups, 1, "fore_pair", sent_g[:1])
    token, backward = finish(kept_g, other_g, g_groups, -1, "back_pair", [token])

    gate_grad = gate_gradient(place, slope, up_sums, back_sums, parts, cols, [token])
    handed_forward, token = collect(forward, "fore_collect")
    (token,) = relay([token], backward[:1], "mark")
    handed_back, _ = collect(backward, "back_collect", [token])
    return handed_forward[None], gate_grad[None], handed_back[None]


def solution(mesh):
    placed = (
        P("section", "col", "row"),
        P("section", None, "col"),
        P("row", "col"),
        P("col", "row"),
        P("section", "col", "row"),
    )
    sizes = mesh.shape
    return jax.shard_map(
        functools.partial(shards, sizes["section"], sizes["col"], sizes["row"]),
        mesh=mesh,
        in_specs=placed,
        out_specs=(
            P("section", "col", "row"),
            P("section", "row", "col"),
            P("section", "col", "row"),
        ),
        check_vma=False,
    )
```
